32 devices in a mesh: rows: 8 (over z, x), vox: 4 (over y, core).
Axes of the slice: x: 2, y: 2, z: 4, core: 2. Of those that a mesh axis runs over, the one named last changes fastest.
Arguments:
- system: float32 [1024, 65536], P('rows', 'vox'), may hold values from -0.0234375 to 0.0234375
- measured: float32 [64, 1024], P(None, 'rows'), may hold values from -18 to 18
- start_image: float32 [64, 65536], P('rows', 'vox'), may hold values from 0 to 1
Outputs:
- image: float32 [64, 65536], P('rows', 'vox')
The draws below stay inside these ranges and needn't reach their ends.
All inputs are finite; a program needn't handle non-finite values.
Results may differ from the reference program's by a relative error of at most 0.0003.
Values sent between devices are 32-bit elements; how exact they have to be, the bound alone decides.
A program may use at most 64 MiB of HBM per device.

```python
import jax
import jax.numpy as jnp
from jax import lax

ROWS_DEV = 128
FRONT = 8
NV = 65536
M = 1024
F = 64
N_ROWS = 8


def block_scale(own_key, shape, cuts, least, largest):
    factor_of = 1.0
    for position, blocks in cuts:
        draws = jax.random.uniform(jax.random.fold_in(jax.random.fold_in(own_key, 6), position), (blocks,), jnp.float32, least / len(cuts), largest / len(cuts))
        factor_of = factor_of * jnp.repeat(jnp.exp(draws), shape[position] // blocks).reshape((-1,) + (1,) * (len(shape) - 1 - position))
    return factor_of


def gaussian(rng, extent, width, most, shards=(), kind=jnp.bfloat16):
    entries = jax.random.normal(rng, extent, jnp.float32) * width
    if len(shards) > 0:
        entries = block_scale(rng, extent, shards, -0.22, 0.18) * entries
    return jnp.clip(entries, min=-most, max=most).astype(kind)


def setup_inputs(seed: int = 0) -> dict:
    key_of = jax.random.split(jax.random.key(seed), 4)
    system = gaussian(key_of[0], (M, NV), NV ** -0.5, 0.0234375, ((0, 8), (1, 4)), jnp.float32)
    measured = gaussian(key_of[1], (F, M), 3.0, 18.0, ((1, 8),), jnp.float32)
    start_image = jnp.clip(1.0 * jax.random.uniform(key_of[2], (F, NV), jnp.float32) ** block_scale(key_of[2], (F, NV), ((0, 8), (1, 4)), -0.2, 0.2), 0.0, 1.0)
    return {"system": system, "measured": measured, "start_image": start_image}


lower_bound = 0.0
upper_bound = 1.0


def reference(system, measured, start_image):
    def one_front(front_index):
        first = (front_index * FRONT).astype(jnp.int32)
        current = lax.dynamic_slice_in_dim(start_image, first, FRONT, 0)
        signals = lax.dynamic_slice_in_dim(measured, first, FRONT, 0)

        def visit(tick_index, current):
            block_index = ((front_index + tick_index) % N_ROWS).astype(jnp.int32)
            offset = (block_index * ROWS_DEV).astype(jnp.int32)
            matrix_tile = lax.dynamic_slice_in_dim(system, offset, ROWS_DEV, 0)
            wanted = lax.dynamic_slice_in_dim(signals, offset, ROWS_DEV, 1)
            product = lax.dot_general(current, matrix_tile, (((1,), (1,)), ((), ())), precision=lax.Precision.HIGHEST)
            residual = wanted - product
            update = jnp.dot(residual, matrix_tile, precision=lax.Precision.HIGHEST)
            return jnp.clip(current + update, lower_bound, upper_bound)

        return lax.fori_loop(0, N_ROWS, visit, current)

    fronts = lax.map(one_front, jnp.arange(N_ROWS, dtype=jnp.int32))
    return fronts.reshape(N_ROWS * FRONT, fronts.shape[2])
```

```python
import functools

import jax
import jax.numpy as jnp
from jax import lax
from jax.experimental import pallas as pl
from jax.experimental.pallas import tpu as pltpu
from jax.sharding import PartitionSpec as P

lower_bound = 0.0
upper_bound = 1.0
HALVES = 2
CHUNKS = 8
EARLY = 5


def split(value):
    high = value.astype(jnp.bfloat16).astype(jnp.float32)
    return high, value - high


def fold(product, rows, cols):
    by_row = product[:rows] + product[rows:]
    return by_row[:, :cols] + by_row[:, cols:]


def kernel(
    cycle, peers, system, measured, start, out,
    landed, tiles, staged, slots, shares, total,
    load_sem, x_sem, sent_sem, got_sem, share_sent, share_got,
):
    me = lax.axis_index("rows")
    mine = lax.axis_index("vox")
    right = lax.rem(me + 1, cycle)
    left = lax.rem(me + cycle - 1, cycle)
    block_rows, voxels = system.shape
    frames = start.shape[0]
    half = frames // HALVES
    width = voxels // CHUNKS
    steps = cycle * HALVES

    def cut(c):
        return pl.ds(c * width, width)

    def load(c):
        return pltpu.make_async_copy(
            system.at[:, cut(c)], landed.at[:, cut(c)], load_sem.at[c]
        )

    fetch = pltpu.make_async_copy(start, staged, x_sem)
    fetch.start()
    for c in range(CHUNKS):
        load(c).start()

    barrier = pltpu.get_barrier_semaphore()
    for neighbour in (left, right):
        pl.semaphore_signal(barrier, inc=1, device_id={"rows": neighbour})
    for away in range(1, peers):
        pl.semaphore_signal(
            barrier, inc=1, device_id={"vox": lax.rem(mine + away, peers)}
        )

    def share_copy(h, away):
        return pltpu.make_async_remote_copy(
            src_ref=shares.at[h, mine],
            dst_ref=shares.at[h, mine],
            send_sem=share_sent.at[h],
            recv_sem=share_got.at[h, mine],
            device_id={"vox": lax.rem(mine + away, peers)},
        )

    def send_share(h, product):
        shares[h, mine] = product
        for away in range(1, peers):
            share_copy(h, away).start()

    def image_copy(h, c):
        return pltpu.make_async_remote_copy(
            src_ref=slots.at[h, :, cut(c)],
            dst_ref=slots.at[h + HALVES, :, cut(c)],
            send_sem=sent_sem.at[h],
            recv_sem=got_sem.at[h + HALVES, c],
            device_id={"rows": right},
        )

    def wait_image(h, c):
        piece = slots.at[h, :, cut(c)]
        pltpu.make_async_copy(piece, piece, got_sem.at[h, c]).wait()

    def wait_sent(h):
        whole = slots.at[h]
        pltpu.make_async_copy(whole, whole, sent_sem.at[h]).wait()
        several = shares.at[h, pl.ds(0, peers - 1)]
        pltpu.make_async_copy(several, several, share_sent.at[h]).wait()

    def stacked(value):
        return jnp.concatenate(split(value), axis=0).astype(jnp.bfloat16)

    def times_tiles(value, c):
        return lax.dot_general(
            stacked(value), tiles[:, cut(c)], (((1,), (1,)), ((), ())),
            preferred_element_type=jnp.float32,
        )

    fetch.wait()
    first = jnp.zeros((2 * frames, 2 * block_rows), jnp.float32)
    for c in range(CHUNKS):
        load(c).wait()
        high, low = split(landed[:, cut(c)])
        tiles[pl.ds(0, block_rows), cut(c)] = high.astype(jnp.bfloat16)
        tiles[pl.ds(block_rows, block_rows), cut(c)] = low.astype(jnp.bfloat16)
        now = staged[:, cut(c)]
        for s in range(HALVES):
            slots[s, :, cut(c)] = now[s * half:(s + 1) * half]
        first += times_tiles(now, c)
    first = fold(first, frames, block_rows)

    pl.semaphore_wait(barrier, 2 + peers - 1)
    for s in range(HALVES):
        send_share(s, first[s * half:(s + 1) * half])

    def step(h, carry):
        tick = h // HALVES
        part = lax.rem(h, HALVES)
        owner = lax.rem(me - tick + cycle, cycle)
        ahead = jnp.logical_and(h > 0, h < steps - 1)

        @pl.when(ahead)
        def _():
            acc = jnp.zeros(total.shape, jnp.float32)
            for c in range(EARLY):
                wait_image(h + 1, c)
                acc += times_tiles(slots[h + 1, :, cut(c)], c)
            total[...] = acc

        for away in range(1, peers):
            source = lax.rem(mine + away, peers)
            piece = shares.at[h, source]
            pltpu.make_async_copy(piece, piece, share_got.at[h, source]).wait()
        summed = shares[h, 0]
        for v in range(1, peers):
            summed += shares[h, v]
        front = measured[pl.ds(pl.multiple_of(owner * frames, frames), frames), :]
        wanted = front[:half]
        for s in range(1, HALVES):
            wanted = jnp.where(part == s, front[s * half:(s + 1) * half], wanted)
        parts = stacked(wanted - summed)
        twice = jnp.concatenate([parts, parts], axis=1)
        for c in range(CHUNKS):
            update = jnp.dot(
                twice, tiles[:, cut(c)], preferred_element_type=jnp.float32
            )
            update = update[:half] + update[half:]
            slots[h, :, cut(c)] = jnp.clip(
                slots[h, :, cut(c)] + update, lower_bound, upper_bound
            )
            image_copy(h, c).start()

        @pl.when(ahead)
        def _():
            acc = total[...]
            for c in range(EARLY, CHUNKS):
                wait_image(h + 1, c)
                acc += times_tiles(slots[h + 1, :, cut(c)], c)
            send_share(h + 1, fold(acc, half, block_rows))

        @pl.when(h >= HALVES)
        def _():
            wait_sent(h - HALVES)

        return carry

    lax.fori_loop(0, steps, step, 0)

    for s in range(HALVES):
        for c in range(CHUNKS):
            wait_image(steps + s, c)
            out[s * half:(s + 1) * half, cut(c)] = slots[steps + s, :, cut(c)]
    for s in range(HALVES):
        wait_sent(steps - HALVES + s)


def shards(system, measured, start_image):
    cycle = lax.axis_size("rows")
    peers = lax.axis_size("vox")
    block_rows, voxels = system.shape
    frames = start_image.shape[0]
    half = frames // HALVES
    steps = cycle * HALVES
    anywhere = pl.BlockSpec(memory_space=pl.ANY)
    near = pl.BlockSpec(memory_space=pltpu.VMEM)
    dma = pltpu.SemaphoreType.DMA
    return pl.pallas_call(
        functools.partial(kernel, cycle, peers),
        out_shape=jax.ShapeDtypeStruct(start_image.shape, start_image.dtype),
        in_specs=[anywhere, near, anywhere],
        out_specs=near,
        scratch_shapes=[
            pltpu.VMEM((block_rows, voxels), jnp.float32),
            pltpu.VMEM((2 * block_rows, voxels), jnp.bfloat16),
            pltpu.VMEM((frames, voxels), jnp.float32),
            pltpu.VMEM((steps + HALVES, half, voxels), jnp.float32),
            pltpu.VMEM((steps, peers, half, block_rows), jnp.float32),
            pltpu.VMEM((2 * half, 2 * block_rows), jnp.float32),
            dma((CHUNKS,)),
            dma,
            dma((steps,)),
            dma((steps + HALVES, CHUNKS)),
            dma((steps,)),
            dma((steps, peers)),
        ],
        compiler_params=pltpu.CompilerParams(
            collective_id=0, has_side_effects=True, vmem_limit_bytes=56 * 2**20
        ),
    )(system, measured, start_image)


def solution(mesh):
    placed = (P("rows", "vox"), P(None, "rows"), P("rows", "vox"))
    return jax.shard_map(
        shards, mesh=mesh, in_specs=placed, out_specs=P("rows", "vox"), check_vma=False
    )
```

```python
import functools

import jax
import jax.numpy as jnp
from jax import lax
from jax.experimental import pallas as pl
from jax.experimental.pallas import tpu as pltpu
from jax.sharding import PartitionSpec as P

lower_bound = 0.0
upper_bound = 1.0
HALVES = 2
CHUNKS = 4
EARLY = 2
LEAD = 4


def split(value):
    high = value.astype(jnp.bfloat16).astype(jnp.float32)
    return high, value - high


def fold(product, rows, cols):
    by_row = product[:rows] + product[rows:]
    return by_row[:, :cols] + by_row[:, cols:]


def kernel(
    cycle, peers, system, measured, start, out,
    landed, tiles, staged, slots, shares, total,
    load_sem, x_sem, sent_sem, got_sem, share_sent, share_got,
):
    me = lax.axis_index("rows")
    mine = lax.axis_index("vox")
    right = lax.rem(me + 1, cycle)
    left = lax.rem(me + cycle - 1, cycle)
    block_rows, voxels = system.shape
    frames = start.shape[0]
    half = frames // HALVES
    width = voxels // CHUNKS
    steps = cycle * HALVES

    def cut(c):
        return pl.ds(c * width, width)

    def load(c):
        return pltpu.make_async_copy(
            system.at[:, cut(c)], landed.at[:, cut(c)], load_sem.at[c]
        )

    fetch = pltpu.make_async_copy(start, staged, x_sem)
    fetch.start()
    for c in range(CHUNKS):
        load(c).start()

    barrier = pltpu.get_barrier_semaphore()
    for neighbour in (left, right):
        pl.semaphore_signal(barrier, inc=1, device_id={"rows": neighbour})
    for away in range(1, peers):
        pl.semaphore_signal(
            barrier, inc=1, device_id={"vox": lax.rem(mine + away, peers)}
        )

    def share_copy(h, away):
        return pltpu.make_async_remote_copy(
            src_ref=shares.at[h, mine],
            dst_ref=shares.at[h, mine],
            send_sem=share_sent.at[h],
            recv_sem=share_got.at[h, mine],
            device_id={"vox": lax.rem(mine + away, peers)},
        )

    def send_share(h, product):
        shares[h, mine] = product
        for away in range(1, peers):
            share_copy(h, away).start()

    def image_copy(h, c):
        return pltpu.make_async_remote_copy(
            src_ref=slots.at[h, :, cut(c)],
            dst_ref=slots.at[h + HALVES, :, cut(c)],
            send_sem=sent_sem.at[h],
            recv_sem=got_sem.at[h + HALVES, c],
            device_id={"rows": right},
        )

    def wait_image(h, c):
        piece = slots.at[h, :, cut(c)]
        pltpu.make_async_copy(piece, piece, got_sem.at[h, c]).wait()

    def wait_sent(h):
        whole = slots.at[h]
        pltpu.make_async_copy(whole, whole, sent_sem.at[h]).wait()
        several = shares.at[h, pl.ds(0, peers - 1)]
        pltpu.make_async_copy(several, several, share_sent.at[h]).wait()

    def stacked(value):
        return jnp.concatenate(split(value), axis=0).astype(jnp.bfloat16)

    def times_tiles(value, c):
        return lax.dot_general(
            stacked(value), tiles[:, cut(c)], (((1,), (1,)), ((), ())),
            preferred_element_type=jnp.float32,
        )

    fetch.wait()
    first = jnp.zeros((2 * frames, 2 * block_rows), jnp.float32)
    for c in range(CHUNKS):
        load(c).wait()
        high, low = split(landed[:, cut(c)])
        tiles[pl.ds(0, block_rows), cut(c)] = high.astype(jnp.bfloat16)
        tiles[pl.ds(block_rows, block_rows), cut(c)] = low.astype(jnp.bfloat16)
        now = staged[:, cut(c)]
        for s in range(HALVES):
            slots[s, :, cut(c)] = now[s * half:(s + 1) * half]
        first += times_tiles(now, c)
    first = fold(first, frames, block_rows)

    pl.semaphore_wait(barrier, 2 + peers - 1)
    for s in range(HALVES):
        send_share(s, first[s * half:(s + 1) * half])

    def step(h, carry):
        tick = h // HALVES
        part = lax.rem(h, HALVES)
        owner = lax.rem(me - tick + cycle, cycle)
        ahead = jnp.logical_and(h > 0, h < steps - 1)

        @pl.when(ahead)
        def _():
            acc = jnp.zeros(total.shape, jnp.float32)
            for c in range(EARLY):
                wait_image(h + 1, c)
                acc += times_tiles(slots[h + 1, :, cut(c)], c)
            total[...] = acc

        for away in range(1, peers):
            source = lax.rem(mine + away, peers)
            piece = shares.at[h, source]
            pltpu.make_async_copy(piece, piece, share_got.at[h, source]).wait()
        summed = shares[h, 0]
        for v in range(1, peers):
            summed += shares[h, v]
        front = measured[pl.ds(pl.multiple_of(owner * frames, frames), frames), :]
        wanted = front[:half]
        for s in range(1, HALVES):
            wanted = jnp.where(part == s, front[s * half:(s + 1) * half], wanted)
        parts = stacked(wanted - summed)
        twice = jnp.concatenate([parts, parts], axis=1)
        def visit(c):
            update = jnp.dot(
                twice, tiles[:, cut(c)], preferred_element_type=jnp.float32
            )
            update = update[:half] + update[half:]
            slots[h, :, cut(c)] = jnp.clip(
                slots[h, :, cut(c)] + update, lower_bound, upper_bound
            )
            image_copy(h, c).start()

        for c in range(LEAD):
            visit(c)

        @pl.when(ahead)
        def _():
            acc = total[...]
            for c in range(EARLY, CHUNKS):
                wait_image(h + 1, c)
                acc += times_tiles(slots[h + 1, :, cut(c)], c)
            send_share(h + 1, fold(acc, half, block_rows))

        for c in range(LEAD, CHUNKS):
            visit(c)

        @pl.when(h >= HALVES)
        def _():
            wait_sent(h - HALVES)

        return carry

    lax.fori_loop(0, steps, step, 0)

    for s in range(HALVES):
        for c in range(CHUNKS):
            wait_image(steps + s, c)
            out[s * half:(s + 1) * half, cut(c)] = slots[steps + s, :, cut(c)]
    for s in range(HALVES):
        wait_sent(steps - HALVES + s)


def shards(system, measured, start_image):
    cycle = lax.axis_size("rows")
    peers = lax.axis_size("vox")
    block_rows, voxels = system.shape
    frames = start_image.shape[0]
    half = frames // HALVES
    steps = cycle * HALVES
    anywhere = pl.BlockSpec(memory_space=pl.ANY)
    near = pl.BlockSpec(memory_space=pltpu.VMEM)
    dma = pltpu.SemaphoreType.DMA
    return pl.pallas_call(
        functools.partial(kernel, cycle, peers),
        out_shape=jax.ShapeDtypeStruct(start_image.shape, start_image.dtype),
        in_specs=[anywhere, near, anywhere],
        out_specs=near,
        scratch_shapes=[
            pltpu.VMEM((block_rows, voxels), jnp.float32),
            pltpu.VMEM((2 * block_rows, voxels), jnp.bfloat16),
            pltpu.VMEM((frames, voxels), jnp.float32),
            pltpu.VMEM((steps + HALVES, half, voxels), jnp.float32),
            pltpu.VMEM((steps, peers, half, block_rows), jnp.float32),
            pltpu.VMEM((2 * half, 2 * block_rows), jnp.float32),
            dma((CHUNKS,)),
            dma,
            dma((steps,)),
            dma((steps + HALVES, CHUNKS)),
            dma((steps,)),
            dma((steps, peers)),
        ],
        compiler_params=pltpu.CompilerParams(
            collective_id=0, has_side_effects=True, vmem_limit_bytes=56 * 2**20
        ),
    )(system, measured, start_image)


def solution(mesh):
    placed = (P("rows", "vox"), P(None, "rows"), P("rows", "vox"))
    return jax.shard_map(
        shards, mesh=mesh, in_specs=placed, out_specs=P("rows", "vox"), check_vma=False
    )
```
